32 devices in a mesh: groups: 2 (over y), row: 4 (over z), col: 4 (over x, core).
Axes of the slice: x: 2, y: 2, z: 4, core: 2. Of those that a mesh axis runs over, the one named last changes fastest.
Arguments:
- inputs: bfloat16 [1024, 8192], P(('groups', 'row'), 'col'), parts along dimension 0, may hold values from -6 to 6
- cotangent: bfloat16 [1024, 8192], P(('groups', 'row'), 'col'), parts along dimension 0, may hold values from -6 to 6
- w_gate: bfloat16 [8192, 14336], P('col', 'row'), may hold values from -0.0625 to 0.0625
- w_up: bfloat16 [8192, 14336], P('col', 'row'), may hold values from -0.0625 to 0.0625
- w_down: bfloat16 [14336, 8192], P('row', 'col'), may hold values from -0.046875 to 0.046875
Outputs:
- output: bfloat16 [1024, 8192], P(('groups', 'row'), 'col'), parts along dimension 0
- d_inputs: bfloat16 [1024, 8192], P(('groups', 'row'), 'col'), parts along dimension 0
- grad_gate: bfloat16 [16384, 14336], P(('groups', 'col'), 'row'), parts along dimension 0
- grad_up: bfloat16 [16384, 14336], P(('groups', 'col'), 'row'), parts along dimension 0
- grad_down: bfloat16 [28672, 8192], P(('groups', 'row'), 'col'), parts along dimension 0
The draws below stay inside these ranges and needn't reach their ends.
There are 2 independent parts, one for each index of `groups`. The reference program is written for one: setup_inputs(seed, part) draws one part's arguments, and reference() takes and returns one part's arrays. A program takes and returns all parts, laid end to end along the dimension named above; an argument that names none is the same for every part. Nothing has to cross between parts.
All inputs are finite; a program needn't handle non-finite values.
Results may differ from the reference program's by a relative error of at most 0.0051.
Values may be sent and summed in bfloat16 or wider, within the bound.
No kernel may reach another device: no remote copies, remote signals or barrier semaphores. Data moves between devices by JAX's collectives and lax.ppermute only.
A program may use at most 256 MiB of HBM per device.

```python
import jax
import jax.numpy as jnp
from jax import lax

D = 8192
FF = 14336
ROWS = 512


def levels(own_key, extent, split, smallest, top_value):
    factor_of = 1.0
    for position, blocks in split:
        steps = jax.random.uniform(jax.random.fold_in(jax.random.fold_in(own_key, 6), position), (blocks,), jnp.float32, smallest / len(split), top_value / len(split))
        factor_of = factor_of * jnp.repeat(jnp.exp(steps), extent[position] // blocks).reshape((-1,) + (1,) * (len(extent) - 1 - position))
    return factor_of


def bell_draw(stream_key, dims, scale, limit, shards=(), dtype=jnp.bfloat16):
    level = levels(stream_key, dims, shards, -0.22, 0.18) if shards else 1.0
    entries = jax.random.normal(stream_key, dims, jnp.float32) * scale * level
    return jnp.minimum(jnp.maximum(entries, -limit), limit).astype(dtype)


def setup_inputs(seed: int = 0, part: int = 0) -> dict:
    arg_keys = jax.random.split(jax.random.key(seed), 6)
    own_keys = jax.random.split(jax.random.fold_in(arg_keys[5], part), 6)
    return {
        "inputs": bell_draw(own_keys[0], (ROWS, D), 1.0, 6.0, ((0, 4), (1, 4))),
        "cotangent": bell_draw(own_keys[1], (ROWS, D), 1.0, 6.0, ((0, 4), (1, 4))),
        "w_gate": bell_draw(arg_keys[2], (D, FF), D ** -0.5, 0.0625, ((0, 4), (1, 4))),
        "w_up": bell_draw(arg_keys[3], (D, FF), D ** -0.5, 0.0625, ((0, 4), (1, 4))),
        "w_down": bell_draw(arg_keys[4], (FF, D), FF ** -0.5, 0.046875, ((0, 4), (1, 4))),
    }


def reference(inputs, cotangent, w_gate, w_up, w_down):
    gate_part = jnp.dot(inputs, w_gate, preferred_element_type=jnp.float32)
    up_part = jnp.dot(inputs, w_up, preferred_element_type=jnp.float32)
    back_grad = lax.dot_general(cotangent, w_down, (((1,), (1,)), ((), ())), preferred_element_type=jnp.float32)
    logistic = jax.nn.sigmoid(gate_part)
    swish = gate_part * logistic
    hidden = (swish * up_part).astype(jnp.bfloat16)
    d_up = (back_grad * swish).astype(jnp.bfloat16)
    d_gate = (back_grad * up_part * logistic * (1.0 + gate_part * (1.0 - logistic))).astype(jnp.bfloat16)
    output = jnp.dot(hidden, w_down, preferred_element_type=jnp.float32).astype(jnp.bfloat16)
    back_in = lax.dot_general(d_gate, w_gate, (((1,), (1,)), ((), ())), preferred_element_type=jnp.float32)
    back_in = back_in + lax.dot_general(d_up, w_up, (((1,), (1,)), ((), ())), preferred_element_type=jnp.float32)
    d_inputs = back_in.astype(jnp.bfloat16)
    contract_rows = (((0,), (0,)), ((), ()))
    grad_down = lax.dot_general(hidden, cotangent, contract_rows, preferred_element_type=jnp.float32).astype(jnp.bfloat16)
    grad_gate = lax.dot_general(inputs, d_gate, contract_rows, preferred_element_type=jnp.float32).astype(jnp.bfloat16)
    grad_up = lax.dot_general(inputs, d_up, contract_rows, preferred_element_type=jnp.float32).astype(jnp.bfloat16)
    return (output, d_inputs, grad_gate, grad_up, grad_down)
```

```python
import jax
import jax.numpy as jnp
from jax import lax
from jax.experimental import pallas as pl
from jax.experimental.pallas import tpu as pltpu
from jax.sharding import PartitionSpec as P

BF16 = jnp.bfloat16
F32 = jnp.float32
NT = (((1,), (1,)), ((), ()))
TN = (((0,), (0,)), ((), ()))
PARAMS = pltpu.CompilerParams(vmem_limit_bytes=66_900_000)
T = 256


def pointwise(gate_part, up_part, back_grad):
    logistic = jax.nn.sigmoid(gate_part)
    swish = gate_part * logistic
    hidden = (swish * up_part).astype(BF16)
    d_up = (back_grad * swish).astype(BF16)
    d_gate = (back_grad * up_part * logistic * (1.0 + gate_part * (1.0 - logistic))).astype(BF16)
    return (hidden, d_gate, d_up)


VMEM = pl.BlockSpec(memory_space=pltpu.VMEM)
SMEM = pl.BlockSpec(memory_space=pltpu.SMEM)
ANY = pl.BlockSpec(memory_space=pltpu.HBM)
DEEP = pl.Buffered(4)


def tile_of(core, tiles, t0, n):
    def tile(j):
        return jnp.where(j < n, (1 - core) * tiles + t0 + j, core * tiles + t0 + j - n)

    return tile


def weight_specs(tile, F, mode):
    return [
        pl.BlockSpec((F, T), lambda j: (0, tile(j)), pipeline_mode=mode),
        pl.BlockSpec((F, T), lambda j: (0, tile(j)), pipeline_mode=mode),
        pl.BlockSpec((T, F), lambda j: (tile(j), 0), pipeline_mode=mode),
    ]


def chain_call(
    name, body, after, args, in_specs, out_shape, out_specs, scratch=(), grid=(), aliases=None
):
    kernel = body
    if after is not None:
        args = list(args) + [after]
        in_specs = list(in_specs) + [ANY]
        count = len(args)

        def kernel(*refs):
            return body(*refs[: count - 1], *refs[count:])

    return pl.pallas_call(
        kernel,
        name=name,
        out_shape=out_shape,
        in_specs=in_specs,
        out_specs=out_specs,
        scratch_shapes=list(scratch),
        grid=grid,
        input_output_aliases=aliases or {},
        compiler_params=PARAMS,
        cost_estimate=pl.CostEstimate(flops=1, bytes_accessed=1, transcendentals=0),
    )(*args)


def forward_call(core, weights, rows, after):
    M, F = rows[0][0].shape[-2:]
    R = M * len(rows)
    n = weights[0].shape[1] // T // 2
    held = [v for some in rows for v in some]

    def body(s, *refs):
        wg_hbm, wu_hbm, wd_hbm, *outs = refs[len(held) : -2]
        x_and_c, sem = refs[-2:]
        tile = tile_of(s[0], n, 0, n)
        copies = []
        at = 0
        for k, some in enumerate(rows):
            for i in range(2):
                source = refs[at + i] if len(some) == 2 else refs[at].at[i]
                copies.append(
                    pltpu.make_async_copy(
                        source, x_and_c.at[i, pl.ds(k * M, M)], sem.at[len(copies)]
                    )
                )
            at += len(some)
        for copy in copies:
            copy.start()
        for copy in copies:
            copy.wait()

        def step(wg, wu, wd, sent_gate, sent_up, sent_back, kept):
            j = pl.program_id(0)

            def sums():
                yield jnp.dot(x_and_c[0], wg[...], preferred_element_type=F32)
                yield jnp.dot(x_and_c[0], wu[...], preferred_element_type=F32)
                yield lax.dot_general(x_and_c[1], wd[...], NT, preferred_element_type=F32)

            @pl.when(j < n)
            def _():
                for out, value in zip((sent_gate, sent_up, sent_back), sums()):
                    out[...] = value.astype(BF16)

            @pl.when(j >= n)
            def _():
                for k, value in enumerate(sums()):
                    kept[k] = value

        pltpu.emit_pipeline(
            step,
            grid=(2 * n,),
            in_specs=weight_specs(tile, F, DEEP),
            out_specs=[pl.BlockSpec((R, T), lambda j: (0, jnp.minimum(j, n - 1)))] * 3
            + [pl.BlockSpec((3, R, T), lambda j: (0, 0, jnp.maximum(j - n, 0)))],
        )(wg_hbm, wu_hbm, wd_hbm, *outs)

    return chain_call(
        "sums",
        body,
        after,
        [core, *held, *weights],
        [SMEM] + [ANY] * (len(held) + 3),
        [jax.ShapeDtypeStruct((R, n * T), BF16)] * 3
        + [jax.ShapeDtypeStruct((3, R, n * T), F32)],
        [ANY] * 4,
        [pltpu.VMEM((2, R, F), BF16), pltpu.SemaphoreType.DMA((2 * len(rows),))],
    )


def hold_call(array, after):
    def body(array_ref, out_ref):
        del array_ref, out_ref

    return chain_call(
        "hold",
        body,
        after,
        [array],
        [ANY],
        jax.ShapeDtypeStruct(array.shape, array.dtype),
        ANY,
        aliases={0: 0},
    )


def half_specs(M, width, k):
    three = pl.BlockSpec((3, M, width // 2), lambda j: (0, k, j))
    one = pl.BlockSpec((M, width // 2), lambda j: (k, j))
    return three, one


def add_call(kept, came, k, M, after):
    width = kept.shape[2]
    three, one = half_specs(M, width, k)

    def body(kept_ref, gate, up, back, send):
        for i, ref in enumerate((gate, up, back)):
            send[i] = (kept_ref[i] + ref[...].astype(F32)).astype(BF16)

    return chain_call(
        "share",
        body,
        after,
        [kept, *came],
        [three, one, one, one],
        jax.ShapeDtypeStruct((3, M, width), BF16),
        half_specs(M, width, 0)[0],
        grid=(2,),
    )


def pointwise_call(kept, came, k, chip, after):
    _, M, width = chip.shape
    three, one = half_specs(M, width, k)
    three_out, one_out = half_specs(M, width, 0)

    def body(kept_ref, gate, up, back, chip_ref, *outs):
        for at in range(0, width // 2, 128):
            cut = slice(at, at + 128)
            sums = [
                kept_ref[i, :, cut] + ref[:, cut].astype(F32) + chip_ref[i, :, cut].astype(F32)
                for i, ref in enumerate((gate, up, back))
            ]
            for out, value in zip(outs, pointwise(*sums)):
                out[:, cut] = value

    return chain_call(
        "point",
        body,
        after,
        [kept, *came, chip],
        [three, one, one, one, three_out],
        [jax.ShapeDtypeStruct((M, width), BF16)] * 3,
        [one_out] * 3,
        grid=(2,),
    )


def results_specs(hs, t0, n, mode):
    specs = []
    for h in hs:
        m = h[0].shape[0]
        specs += [pl.BlockSpec((m, T), lambda j: (0, t0 + jnp.minimum(j, n - 1)), pipeline_mode=mode)] * 3
        specs += [pl.BlockSpec((m, T), lambda j: (0, t0 + jnp.maximum(j - n, 0)), pipeline_mode=mode)] * 3
    return specs


def each_half(n, refs, work):
    j = pl.program_id(0)

    def rows(lo):
        return [
            jnp.concatenate([refs[at + lo + k][...] for at in range(0, len(refs), 6)], axis=0)
            for k in range(3)
        ]

    @pl.when(j < n)
    def _():
        work(*rows(0))

    @pl.when(j >= n)
    def _():
        work(*rows(3))


def backward_call(core, weights, span, hs, dtypes, after):
    t0, n = span
    F = weights[0].shape[0]
    tiles = weights[0].shape[1] // T // 2
    M = hs[0][0].shape[0]
    R = M * len(hs)

    def body(s, wg_hbm, wu_hbm, wd_hbm, *refs):
        h_hbm = refs[: 6 * len(hs)]
        *outs, acc = refs[6 * len(hs) :]
        tile = tile_of(s[0], tiles, t0, n)
        acc[...] = jnp.zeros_like(acc)

        def step(wg, wu, wd, *h):
            def work(hid, dg, du):
                acc[0] += jnp.dot(hid, wd[...], preferred_element_type=F32)
                acc[1] += lax.dot_general(
                    dg, wg[...], NT, preferred_element_type=F32
                ) + lax.dot_general(du, wu[...], NT, preferred_element_type=F32)

            each_half(n, h, work)

        pltpu.emit_pipeline(
            step,
            grid=(2 * n,),
            in_specs=weight_specs(tile, F, DEEP) + results_specs(hs, t0, n, DEEP),
        )(wg_hbm, wu_hbm, wd_hbm, *h_hbm)
        for k, out in enumerate(outs):
            out[...] = acc[:, k * M : (k + 1) * M].astype(out.dtype)

    flat = [v for h in hs for v in h]
    return chain_call(
        "back",
        body,
        after,
        [core, *weights, *flat],
        [SMEM] + [ANY] * (3 + len(flat)),
        [jax.ShapeDtypeStruct((2, M, F), dtype) for dtype in dtypes],
        [VMEM] * len(hs),
        [pltpu.VMEM((2, R, F), F32)],
    )


def join_call(part, came, split, after):
    _, M, F = part.shape
    both = pl.BlockSpec((2, M // 2, F), lambda j: (0, j, 0))

    def body(part_ref, came_ref, *outs):
        for i in range(2):
            value = (part_ref[i] + came_ref[i].astype(F32)).astype(BF16)
            if split:
                outs[i][...] = value
            else:
                outs[0][i] = value

    if split:
        shapes, specs = [(M, F)] * 2, [pl.BlockSpec((M // 2, F), lambda j: (j, 0))] * 2
    else:
        shapes, specs = [(2, M, F)], [both]
    return chain_call(
        "join",
        body,
        after,
        [part, came],
        [both, both],
        [jax.ShapeDtypeStruct(shape, BF16) for shape in shapes],
        specs,
        grid=(2,),
    )


def grads_call(core, span, rows, hs, shapes, after):
    t0, n = span
    R = len(rows)
    M, F = rows[0][0].shape[-2:]
    held = [v for some in rows for v in some]
    tiles = shapes[0][1] // T // 2

    def body(s, *refs):
        h_hbm = refs[len(held) : len(held) + 6 * R]
        gate_hbm, up_hbm, down_hbm, x_rows, c_rows, x_in, sem = refs[len(held) + 6 * R :]
        tile = tile_of(s[0], tiles, t0, n)
        copies = []
        at = 0
        for k, some in enumerate(rows):
            x, c = (refs[at], refs[at + 1]) if len(some) == 2 else (refs[at].at[0], refs[at].at[1])
            at += len(some)
            copies.append(pltpu.make_async_copy(x, x_in.at[k], sem.at[k]))
            copies.append(pltpu.make_async_copy(c, c_rows.at[pl.ds(k * M, M)], sem.at[R + k]))
        for copy in copies[::2] + copies[1::2]:
            copy.start()
        for k in range(R):
            copies[2 * k].wait()
            x_rows[:, k * M : (k + 1) * M] = x_in[k].T
        for copy in copies[1::2]:
            copy.wait()

        def step(*h):
            h, (gate, up, down) = h[:-3], h[-3:]

            def work(hid, dg, du):
                gate[...] = jnp.dot(x_rows[...], dg, preferred_element_type=F32).astype(BF16)
                up[...] = jnp.dot(x_rows[...], du, preferred_element_type=F32).astype(BF16)
                down[...] = lax.dot_general(
                    hid, c_rows[...], TN, preferred_element_type=F32
                ).astype(BF16)

            each_half(n, h, work)

        pltpu.emit_pipeline(
            step,
            grid=(2 * n,),
            in_specs=results_specs(hs, t0, n, None),
            out_specs=weight_specs(tile, F, None),
        )(*h_hbm, gate_hbm, up_hbm, down_hbm)

    flat = [v for h in hs for v in h]
    return chain_call(
        "grads",
        body,
        after,
        [core, *held, *flat],
        [SMEM] + [ANY] * (len(held) + len(flat)),
        [jax.ShapeDtypeStruct(s, BF16) for s in shapes],
        [ANY] * 3,
        [
            pltpu.VMEM((F, R * M), BF16),
            pltpu.VMEM((R * M, F), BF16),
            pltpu.VMEM((R, M, F), BF16),
            pltpu.SemaphoreType.DMA((2 * R,)),
        ],
    )


ORDER = ["S0", "A0", "W1", "S1", "W2", "A1", "S2", "P0", "A2", "S3", "P1", "A3", "B01", "P2", "B2"]
ORDER += ["J2", "P3", "B3", "J3", "G", "J0"]


def tiled(rows, cols):
    def local(inputs, cotangent, w_gate, w_up, w_down):
        weights = (w_gate, w_up, w_down)
        shapes = [w.shape for w in weights]
        full = (0, w_gate.shape[1] // T // 2)
        core = (lax.axis_index("col") % 2).astype(jnp.int32).reshape(1)
        to_core = lambda v: lax.ppermute(v, "col", [(i, i ^ 1) for i in range(cols)])
        to_chip = lambda v: lax.ppermute(v, "col", [(i, i ^ 2) for i in range(cols)])
        onward = lambda v: lax.ppermute(v, "row", [(i, (i + 1) % rows) for i in range(rows)])
        last = [None]

        def then(call, *args):
            out = call(*args, last[0])
            last[0] = out[0] if isinstance(out, (list, tuple)) else out
            return out

        held = [(inputs, cotangent), (onward(jnp.stack([inputs, cotangent])),)]

        M = inputs.shape[0]
        kept, came, block, chip, h, totals = {}, {}, {}, {}, {}, {}
        for word in ORDER:
            step, digits = word[0], [int(d) for d in word[1:]]
            k = digits[0] if digits else None
            if step == "S":
                *sent, own = then(forward_call, core, weights, [held[k] for k in digits])
                sent = [to_core(v) for v in sent]
                for at, k in enumerate(digits):
                    kept[k], came[k], block[k] = own, sent, at
            elif step == "W":
                held[k] = (then(hold_call, held[k][0]),)
                held.append((onward(held[k][0]),))
            elif step == "A":
                chip[k] = to_chip(then(add_call, kept[k], came[k], block[k], M))
            elif step == "P":
                own = then(pointwise_call, kept[k], came[k], block[k], chip[k])
                h[k] = [to_core(v) for v in own] + list(own)
            elif step == "B":
                dtypes = [BF16 if k == 1 else F32 for k in digits]
                sums = then(backward_call, core, weights, full, [h[k] for k in digits], dtypes)
                totals.update(zip(digits, sums))
                if 1 in digits:
                    moving = onward(totals[1])
            elif step == "J" and k:
                moving = onward(*then(join_call, totals[k], moving, False))
            elif step == "J":
                output, d_inputs = then(join_call, totals[0], moving, True)
            elif step == "G":
                grads = then(grads_call, core, full, held, [h[k] for k in range(rows)], shapes)
        return (output, d_inputs, *grads)

    return local


def plain(inputs, cotangent, w_gate, w_up, w_down):
    full_inputs, full_cotangent = (
        lax.all_gather(inputs, "row", axis=0, tiled=True),
        lax.all_gather(cotangent, "row", axis=0, tiled=True),
    )
    hidden_width = w_gate.shape[1]
    feature_width = w_down.shape[1]
    gate_part = jnp.dot(full_inputs, w_gate, preferred_element_type=F32)
    up_part = jnp.dot(full_inputs, w_up, preferred_element_type=F32)
    back_grad = lax.dot_general(full_cotangent, w_down, NT, preferred_element_type=F32)
    shares = lax.psum_scatter(
        jnp.concatenate([gate_part, up_part, back_grad], axis=1),
        "col",
        scatter_dimension=0,
        tiled=True,
    )
    hidden, d_gate, d_up = (
        lax.all_gather(share, "col", axis=0, tiled=True)
        for share in pointwise(
            shares[:, :hidden_width],
            shares[:, hidden_width : 2 * hidden_width],
            shares[:, 2 * hidden_width :],
        )
    )
    grad_down = lax.dot_general(hidden, full_cotangent, TN, preferred_element_type=F32)
    grad_gate = lax.dot_general(full_inputs, d_gate, TN, preferred_element_type=F32)
    grad_up = lax.dot_general(full_inputs, d_up, TN, preferred_element_type=F32)
    forward_term = jnp.dot(hidden, w_down, preferred_element_type=F32)
    back_term = lax.dot_general(d_gate, w_gate, NT, preferred_element_type=F32)
    back_term = back_term + lax.dot_general(d_up, w_up, NT, preferred_element_type=F32)
    results = lax.psum_scatter(
        jnp.concatenate([forward_term, back_term], axis=1), "row", scatter_dimension=0, tiled=True
    )
    return (
        results[:, :feature_width].astype(BF16),
        results[:, feature_width:].astype(BF16),
        grad_gate.astype(BF16),
        grad_up.astype(BF16),
        grad_down.astype(BF16),
    )


def solution(mesh):
    rows, cols = mesh.shape["row"], mesh.shape["col"]

    def local(inputs, cotangent, w_gate, w_up, w_down):
        step = plain
        if rows == 4 and cols == 4 and w_gate.shape[1] % (14 * T) == 0 and inputs.shape[0] % 16 == 0:
            step = tiled(rows, cols)
        return step(inputs, cotangent, w_gate, w_up, w_down)

    return jax.shard_map(
        local,
        mesh=mesh,
        in_specs=(
            P(("groups", "row"), "col"),
            P(("groups", "row"), "col"),
            P("col", "row"),
            P("col", "row"),
            P("row", "col"),
        ),
        out_specs=(
            P(("groups", "row"), "col"),
            P(("groups", "row"), "col"),
            P(("groups", "col"), "row"),
            P(("groups", "col"), "row"),
            P(("groups", "row"), "col"),
        ),
        check_vma=False,
    )
```

```python
import jax
import jax.numpy as jnp
from jax import lax
from jax.experimental import pallas as pl
from jax.experimental.pallas import tpu as pltpu
from jax.sharding import PartitionSpec as P

BF16 = jnp.bfloat16
F32 = jnp.float32
NT = (((1,), (1,)), ((), ()))
TN = (((0,), (0,)), ((), ()))
PARAMS = pltpu.CompilerParams(vmem_limit_bytes=66_900_000)
T = 256


def pointwise(gate_part, up_part, back_grad):
    logistic = jax.nn.sigmoid(gate_part)
    swish = gate_part * logistic
    hidden = (swish * up_part).astype(BF16)
    d_up = (back_grad * swish).astype(BF16)
    d_gate = (back_grad * up_part * logistic * (1.0 + gate_part * (1.0 - logistic))).astype(BF16)
    return (hidden, d_gate, d_up)


VMEM = pl.BlockSpec(memory_space=pltpu.VMEM)
SMEM = pl.BlockSpec(memory_space=pltpu.SMEM)
ANY = pl.BlockSpec(memory_space=pltpu.HBM)
DEEP = pl.Buffered(4)


def tile_of(core, tiles, t0, n):
    def tile(j):
        return jnp.where(j < n, (1 - core) * tiles + t0 + j, core * tiles + t0 + j - n)

    return tile


def weight_specs(tile, F, mode):
    return [
        pl.BlockSpec((F, T), lambda j: (0, tile(j)), pipeline_mode=mode),
        pl.BlockSpec((F, T), lambda j: (0, tile(j)), pipeline_mode=mode),
        pl.BlockSpec((T, F), lambda j: (tile(j), 0), pipeline_mode=mode),
    ]


def chain_call(
    name, body, after, args, in_specs, out_shape, out_specs, scratch=(), grid=(), aliases=None
):
    kernel = body
    if after is not None:
        args = list(args) + [after]
        in_specs = list(in_specs) + [ANY]
        count = len(args)

        def kernel(*refs):
            return body(*refs[: count - 1], *refs[count:])

    return pl.pallas_call(
        kernel,
        name=name,
        out_shape=out_shape,
        in_specs=in_specs,
        out_specs=out_specs,
        scratch_shapes=list(scratch),
        grid=grid,
        input_output_aliases=aliases or {},
        compiler_params=PARAMS,
        cost_estimate=pl.CostEstimate(flops=1, bytes_accessed=1, transcendentals=0),
    )(*args)


def forward_call(core, weights, rows, after):
    M, F = rows[0][0].shape[-2:]
    R = M * len(rows)
    n = weights[0].shape[1] // T // 2
    held = [v for some in rows for v in some]

    def body(s, *refs):
        wg_hbm, wu_hbm, wd_hbm, *outs = refs[len(held) : -2]
        x_and_c, sem = refs[-2:]
        tile = tile_of(s[0], n, 0, n)
        copies = []
        at = 0
        for k, some in enumerate(rows):
            for i in range(2):
                source = refs[at + i] if len(some) == 2 else refs[at].at[i]
                copies.append(
                    pltpu.make_async_copy(
                        source, x_and_c.at[i, pl.ds(k * M, M)], sem.at[len(copies)]
                    )
                )
            at += len(some)
        for copy in copies:
            copy.start()
        for copy in copies:
            copy.wait()

        def step(wg, wu, wd, sent_gate, sent_up, sent_back, kept):
            j = pl.program_id(0)

            def sums():
                yield jnp.dot(x_and_c[0], wg[...], preferred_element_type=F32)
                yield jnp.dot(x_and_c[0], wu[...], preferred_element_type=F32)
                yield lax.dot_general(x_and_c[1], wd[...], NT, preferred_element_type=F32)

            @pl.when(j < n)
            def _():
                for out, value in zip((sent_gate, sent_up, sent_back), sums()):
                    out[...] = value.astype(BF16)

            @pl.when(j >= n)
            def _():
                for k, value in enumerate(sums()):
                    kept[k] = value

        pltpu.emit_pipeline(
            step,
            grid=(2 * n,),
            in_specs=weight_specs(tile, F, DEEP),
            out_specs=[pl.BlockSpec((R, T), lambda j: (0, jnp.minimum(j, n - 1)))] * 3
            + [pl.BlockSpec((3, R, T), lambda j: (0, 0, jnp.maximum(j - n, 0)))],
        )(wg_hbm, wu_hbm, wd_hbm, *outs)

    return chain_call(
        "sums",
        body,
        after,
        [core, *held, *weights],
        [SMEM] + [ANY] * (len(held) + 3),
        [jax.ShapeDtypeStruct((R, n * T), BF16)] * 3
        + [jax.ShapeDtypeStruct((3, R, n * T), F32)],
        [ANY] * 4,
        [pltpu.VMEM((2, R, F), BF16), pltpu.SemaphoreType.DMA((2 * len(rows),))],
    )


def hold_call(array, after):
    def body(array_ref, out_ref):
        del array_ref, out_ref

    return chain_call(
        "hold",
        body,
        after,
        [array],
        [ANY],
        jax.ShapeDtypeStruct(array.shape, array.dtype),
        ANY,
        aliases={0: 0},
    )


def half_specs(M, width, k):
    three = pl.BlockSpec((3, M, width // 2), lambda j: (0, k, j))
    one = pl.BlockSpec((M, width // 2), lambda j: (k, j))
    return three, one


def add_call(kept, came, k, M, after):
    width = kept.shape[2]
    three, one = half_specs(M, width, k)

    def body(kept_ref, gate, up, back, send):
        for i, ref in enumerate((gate, up, back)):
            send[i] = (kept_ref[i] + ref[...].astype(F32)).astype(BF16)

    return chain_call(
        "share",
        body,
        after,
        [kept, *came],
        [three, one, one, one],
        jax.ShapeDtypeStruct((3, M, width), BF16),
        half_specs(M, width, 0)[0],
        grid=(2,),
    )


def pointwise_call(kept, came, k, chip, after):
    _, M, width = chip.shape
    three, one = half_specs(M, width, k)
    three_out, one_out = half_specs(M, width, 0)

    def body(kept_ref, gate, up, back, chip_ref, *outs):
        for at in range(0, width // 2, 128):
            cut = slice(at, at + 128)
            sums = [
                kept_ref[i, :, cut] + ref[:, cut].astype(F32) + chip_ref[i, :, cut].astype(F32)
                for i, ref in enumerate((gate, up, back))
            ]
            for out, value in zip(outs, pointwise(*sums)):
                out[:, cut] = value

    return chain_call(
        "point",
        body,
        after,
        [kept, *came, chip],
        [three, one, one, one, three_out],
        [jax.ShapeDtypeStruct((M, width), BF16)] * 3,
        [one_out] * 3,
        grid=(2,),
    )


def results_specs(hs, t0, n, mode):
    specs = []
    for h in hs:
        m = h[0].shape[0]
        specs += [pl.BlockSpec((m, T), lambda j: (0, t0 + jnp.minimum(j, n - 1)), pipeline_mode=mode)] * 3
        specs += [pl.BlockSpec((m, T), lambda j: (0, t0 + jnp.maximum(j - n, 0)), pipeline_mode=mode)] * 3
    return specs


def each_half(n, refs, work):
    j = pl.program_id(0)

    def rows(lo):
        return [
            jnp.concatenate([refs[at + lo + k][...] for at in range(0, len(refs), 6)], axis=0)
            for k in range(3)
        ]

    @pl.when(j < n)
    def _():
        work(*rows(0))

    @pl.when(j >= n)
    def _():
        work(*rows(3))


def backward_call(core, weights, span, hs, dtypes, after):
    t0, n = span
    F = weights[0].shape[0]
    tiles = weights[0].shape[1] // T // 2
    M = hs[0][0].shape[0]
    R = M * len(hs)

    def body(s, wg_hbm, wu_hbm, wd_hbm, *refs):
        h_hbm = refs[: 6 * len(hs)]
        *outs, acc = refs[6 * len(hs) :]
        tile = tile_of(s[0], tiles, t0, n)
        acc[...] = jnp.zeros_like(acc)

        def step(wg, wu, wd, *h):
            def work(hid, dg, du):
                acc[0] += jnp.dot(hid, wd[...], preferred_element_type=F32)
                acc[1] += lax.dot_general(
                    dg, wg[...], NT, preferred_element_type=F32
                ) + lax.dot_general(du, wu[...], NT, preferred_element_type=F32)

            each_half(n, h, work)

        pltpu.emit_pipeline(
            step,
            grid=(2 * n,),
            in_specs=weight_specs(tile, F, DEEP) + results_specs(hs, t0, n, DEEP),
        )(wg_hbm, wu_hbm, wd_hbm, *h_hbm)
        for k, out in enumerate(outs):
            out[...] = acc[:, k * M : (k + 1) * M].astype(out.dtype)

    flat = [v for h in hs for v in h]
    return chain_call(
        "back",
        body,
        after,
        [core, *weights, *flat],
        [SMEM] + [ANY] * (3 + len(flat)),
        [jax.ShapeDtypeStruct((2, M, F), dtype) for dtype in dtypes],
        [VMEM] * len(hs),
        [pltpu.VMEM((2, R, F), F32)],
    )


def join_call(part, came, split, after):
    _, M, F = part.shape
    both = pl.BlockSpec((2, M // 2, F), lambda j: (0, j, 0))

    def body(part_ref, came_ref, *outs):
        for i in range(2):
            value = (part_ref[i] + came_ref[i].astype(F32)).astype(BF16)
            if split:
                outs[i][...] = value
            else:
                outs[0][i] = value

    if split:
        shapes, specs = [(M, F)] * 2, [pl.BlockSpec((M // 2, F), lambda j: (j, 0))] * 2
    else:
        shapes, specs = [(2, M, F)], [both]
    return chain_call(
        "join",
        body,
        after,
        [part, came],
        [both, both],
        [jax.ShapeDtypeStruct(shape, BF16) for shape in shapes],
        specs,
        grid=(2,),
    )


def grads_call(core, span, rows, hs, shapes, after):
    t0, n = span
    R = len(rows)
    M, F = rows[0][0].shape[-2:]
    held = [v for some in rows for v in some]
    tiles = shapes[0][1] // T // 2

    def body(s, *refs):
        h_hbm = refs[len(held) : len(held) + 6 * R]
        gate_hbm, up_hbm, down_hbm, x_rows, c_rows, x_in, sem = refs[len(held) + 6 * R :]
        tile = tile_of(s[0], tiles, t0, n)
        copies = []
        at = 0
        for k, some in enumerate(rows):
            x, c = (refs[at], refs[at + 1]) if len(some) == 2 else (refs[at].at[0], refs[at].at[1])
            at += len(some)
            copies.append(pltpu.make_async_copy(x, x_in.at[k], sem.at[k]))
            copies.append(pltpu.make_async_copy(c, c_rows.at[pl.ds(k * M, M)], sem.at[R + k]))
        for copy in copies[::2] + copies[1::2]:
            copy.start()
        for k in range(R):
            copies[2 * k].wait()
            x_rows[:, k * M : (k + 1) * M] = x_in[k].T
        for copy in copies[1::2]:
            copy.wait()

        def step(*h):
            h, (gate, up, down) = h[:-3], h[-3:]

            def work(hid, dg, du):
                gate[...] = jnp.dot(x_rows[...], dg, preferred_element_type=F32).astype(BF16)
                up[...] = jnp.dot(x_rows[...], du, preferred_element_type=F32).astype(BF16)
                down[...] = lax.dot_general(
                    hid, c_rows[...], TN, preferred_element_type=F32
                ).astype(BF16)

            each_half(n, h, work)

        pltpu.emit_pipeline(
            step,
            grid=(2 * n,),
            in_specs=results_specs(hs, t0, n, None),
            out_specs=weight_specs(tile, F, None),
        )(*h_hbm, gate_hbm, up_hbm, down_hbm)

    flat = [v for h in hs for v in h]
    return chain_call(
        "grads",
        body,
        after,
        [core, *held, *flat],
        [SMEM] + [ANY] * (len(held) + len(flat)),
        [jax.ShapeDtypeStruct(s, BF16) for s in shapes],
        [ANY] * 3,
        [
            pltpu.VMEM((F, R * M), BF16),
            pltpu.VMEM((R * M, F), BF16),
            pltpu.VMEM((R, M, F), BF16),
            pltpu.SemaphoreType.DMA((2 * R,)),
        ],
    )


ORDER = ["S0", "A0", "W1", "S1", "A1", "W2", "S2", "P0", "A2", "S3", "P1", "A3", "B01", "P2", "B2"]
ORDER += ["J2", "P3", "B3", "J3", "G", "J0"]


def tiled(rows, cols):
    def local(inputs, cotangent, w_gate, w_up, w_down):
        weights = (w_gate, w_up, w_down)
        shapes = [w.shape for w in weights]
        full = (0, w_gate.shape[1] // T // 2)
        core = (lax.axis_index("col") % 2).astype(jnp.int32).reshape(1)
        to_core = lambda v: lax.ppermute(v, "col", [(i, i ^ 1) for i in range(cols)])
        to_chip = lambda v: lax.ppermute(v, "col", [(i, i ^ 2) for i in range(cols)])
        onward = lambda v: lax.ppermute(v, "row", [(i, (i + 1) % rows) for i in range(rows)])
        last = [None]

        def then(call, *args):
            out = call(*args, last[0])
            last[0] = out[0] if isinstance(out, (list, tuple)) else out
            return out

        held = [(inputs, cotangent), (onward(jnp.stack([inputs, cotangent])),)]

        M = inputs.shape[0]
        kept, came, block, chip, h, totals = {}, {}, {}, {}, {}, {}
        for word in ORDER:
            step, digits = word[0], [int(d) for d in word[1:]]
            k = digits[0] if digits else None
            if step == "S":
                *sent, own = then(forward_call, core, weights, [held[k] for k in digits])
                sent = [to_core(v) for v in sent]
                for at, k in enumerate(digits):
                    kept[k], came[k], block[k] = own, sent, at
            elif step == "W":
                held[k] = (then(hold_call, held[k][0]),)
                held.append((onward(held[k][0]),))
            elif step == "A":
                chip[k] = to_chip(then(add_call, kept[k], came[k], block[k], M))
            elif step == "P":
                own = then(pointwise_call, kept[k], came[k], block[k], chip[k])
                h[k] = [to_core(v) for v in own] + list(own)
            elif step == "B":
                dtypes = [BF16 if k == 1 else F32 for k in digits]
                sums = then(backward_call, core, weights, full, [h[k] for k in digits], dtypes)
                totals.update(zip(digits, sums))
                if 1 in digits:
                    moving = onward(totals[1])
            elif step == "J" and k:
                moving = onward(*then(join_call, totals[k], moving, False))
            elif step == "J":
                output, d_inputs = then(join_call, totals[0], moving, True)
            elif step == "G":
                grads = then(grads_call, core, full, held, [h[k] for k in range(rows)], shapes)
        return (output, d_inputs, *grads)

    return local


def plain(inputs, cotangent, w_gate, w_up, w_down):
    full_inputs, full_cotangent = (
        lax.all_gather(inputs, "row", axis=0, tiled=True),
        lax.all_gather(cotangent, "row", axis=0, tiled=True),
    )
    hidden_width = w_gate.shape[1]
    feature_width = w_down.shape[1]
    gate_part = jnp.dot(full_inputs, w_gate, preferred_element_type=F32)
    up_part = jnp.dot(full_inputs, w_up, preferred_element_type=F32)
    back_grad = lax.dot_general(full_cotangent, w_down, NT, preferred_element_type=F32)
    shares = lax.psum_scatter(
        jnp.concatenate([gate_part, up_part, back_grad], axis=1),
        "col",
        scatter_dimension=0,
        tiled=True,
    )
    hidden, d_gate, d_up = (
        lax.all_gather(share, "col", axis=0, tiled=True)
        for share in pointwise(
            shares[:, :hidden_width],
            shares[:, hidden_width : 2 * hidden_width],
            shares[:, 2 * hidden_width :],
        )
    )
    grad_down = lax.dot_general(hidden, full_cotangent, TN, preferred_element_type=F32)
    grad_gate = lax.dot_general(full_inputs, d_gate, TN, preferred_element_type=F32)
    grad_up = lax.dot_general(full_inputs, d_up, TN, preferred_element_type=F32)
    forward_term = jnp.dot(hidden, w_down, preferred_element_type=F32)
    back_term = lax.dot_general(d_gate, w_gate, NT, preferred_element_type=F32)
    back_term = back_term + lax.dot_general(d_up, w_up, NT, preferred_element_type=F32)
    results = lax.psum_scatter(
        jnp.concatenate([forward_term, back_term], axis=1), "row", scatter_dimension=0, tiled=True
    )
    return (
        results[:, :feature_width].astype(BF16),
        results[:, feature_width:].astype(BF16),
        grad_gate.astype(BF16),
        grad_up.astype(BF16),
        grad_down.astype(BF16),
    )


def solution(mesh):
    rows, cols = mesh.shape["row"], mesh.shape["col"]

    def local(inputs, cotangent, w_gate, w_up, w_down):
        step = plain
        if rows == 4 and cols == 4 and w_gate.shape[1] % (14 * T) == 0 and inputs.shape[0] % 16 == 0:
            step = tiled(rows, cols)
        return step(inputs, cotangent, w_gate, w_up, w_down)

    return jax.shard_map(
        local,
        mesh=mesh,
        in_specs=(
            P(("groups", "row"), "col"),
            P(("groups", "row"), "col"),
            P("col", "row"),
            P("col", "row"),
            P("row", "col"),
        ),
        out_specs=(
            P(("groups", "row"), "col"),
            P(("groups", "row"), "col"),
            P(("groups", "col"), "row"),
            P(("groups", "col"), "row"),
            P(("groups", "row"), "col"),
        ),
        check_vma=False,
    )
```

```python
import jax
import jax.numpy as jnp
from jax import lax
from jax.experimental import pallas as pl
from jax.experimental.pallas import tpu as pltpu
from jax.sharding import PartitionSpec as P

BF16 = jnp.bfloat16
F32 = jnp.float32
NT = (((1,), (1,)), ((), ()))
TN = (((0,), (0,)), ((), ()))
PARAMS = pltpu.CompilerParams(vmem_limit_bytes=66_900_000)
T = 256


def pointwise(gate_part, up_part, back_grad):
    logistic = jax.nn.sigmoid(gate_part)
    swish = gate_part * logistic
    hidden = (swish * up_part).astype(BF16)
    d_up = (back_grad * swish).astype(BF16)
    d_gate = (back_grad * up_part * logistic * (1.0 + gate_part * (1.0 - logistic))).astype(BF16)
    return (hidden, d_gate, d_up)


VMEM = pl.BlockSpec(memory_space=pltpu.VMEM)
SMEM = pl.BlockSpec(memory_space=pltpu.SMEM)
ANY = pl.BlockSpec(memory_space=pltpu.HBM)
DEEP = pl.Buffered(4)


def tile_of(core, tiles, t0, n):
    def tile(j):
        return jnp.where(j < n, (1 - core) * tiles + t0 + j, core * tiles + t0 + j - n)

    return tile


def weight_specs(tile, F, mode):
    return [
        pl.BlockSpec((F, T), lambda j: (0, tile(j)), pipeline_mode=mode),
        pl.BlockSpec((F, T), lambda j: (0, tile(j)), pipeline_mode=mode),
        pl.BlockSpec((T, F), lambda j: (tile(j), 0), pipeline_mode=mode),
    ]


def chain_call(
    name, body, after, args, in_specs, out_shape, out_specs, scratch=(), grid=(), aliases=None
):
    kernel = body
    if after is not None:
        args = list(args) + [after]
        in_specs = list(in_specs) + [ANY]
        count = len(args)

        def kernel(*refs):
            return body(*refs[: count - 1], *refs[count:])

    return pl.pallas_call(
        kernel,
        name=name,
        out_shape=out_shape,
        in_specs=in_specs,
        out_specs=out_specs,
        scratch_shapes=list(scratch),
        grid=grid,
        input_output_aliases=aliases or {},
        compiler_params=PARAMS,
        cost_estimate=pl.CostEstimate(flops=1, bytes_accessed=1, transcendentals=0),
    )(*args)


def forward_call(core, weights, rows, after):
    M, F = rows[0][0].shape[-2:]
    R = M * len(rows)
    n = weights[0].shape[1] // T // 2
    held = [v for some in rows for v in some]

    def body(s, *refs):
        wg_hbm, wu_hbm, wd_hbm, *outs = refs[len(held) : -2]
        x_and_c, sem = refs[-2:]
        tile = tile_of(s[0], n, 0, n)
        copies = []
        at = 0
        for k, some in enumerate(rows):
            for i in range(2):
                source = refs[at + i] if len(some) == 2 else refs[at].at[i]
                copies.append(
                    pltpu.make_async_copy(
                        source, x_and_c.at[i, pl.ds(k * M, M)], sem.at[len(copies)]
                    )
                )
            at += len(some)
        for copy in copies:
            copy.start()
        for copy in copies:
            copy.wait()

        def step(wg, wu, wd, sent_gate, sent_up, sent_back, kept):
            j = pl.program_id(0)

            def sums():
                yield jnp.dot(x_and_c[0], wg[...], preferred_element_type=F32)
                yield jnp.dot(x_and_c[0], wu[...], preferred_element_type=F32)
                yield lax.dot_general(x_and_c[1], wd[...], NT, preferred_element_type=F32)

            @pl.when(j < n)
            def _():
                for out, value in zip((sent_gate, sent_up, sent_back), sums()):
                    out[...] = value.astype(BF16)

            @pl.when(j >= n)
            def _():
                for k, value in enumerate(sums()):
                    kept[k] = value

        pltpu.emit_pipeline(
            step,
            grid=(2 * n,),
            in_specs=weight_specs(tile, F, DEEP),
            out_specs=[pl.BlockSpec((R, T), lambda j: (0, jnp.minimum(j, n - 1)))] * 3
            + [pl.BlockSpec((3, R, T), lambda j: (0, 0, jnp.maximum(j - n, 0)))],
        )(wg_hbm, wu_hbm, wd_hbm, *outs)

    return chain_call(
        "sums",
        body,
        after,
        [core, *held, *weights],
        [SMEM] + [ANY] * (len(held) + 3),
        [jax.ShapeDtypeStruct((R, n * T), BF16)] * 3
        + [jax.ShapeDtypeStruct((3, R, n * T), F32)],
        [ANY] * 4,
        [pltpu.VMEM((2, R, F), BF16), pltpu.SemaphoreType.DMA((2 * len(rows),))],
    )


def hold_call(array, after):
    def body(array_ref, out_ref):
        del array_ref, out_ref

    return chain_call(
        "hold",
        body,
        after,
        [array],
        [ANY],
        jax.ShapeDtypeStruct(array.shape, array.dtype),
        ANY,
        aliases={0: 0},
    )


def half_specs(M, width, k):
    three = pl.BlockSpec((3, M, width // 2), lambda j: (0, k, j))
    one = pl.BlockSpec((M, width // 2), lambda j: (k, j))
    return three, one


def add_call(kept, came, k, M, after):
    width = kept.shape[2]
    three, one = half_specs(M, width, k)

    def body(kept_ref, gate, up, back, send):
        for i, ref in enumerate((gate, up, back)):
            send[i] = (kept_ref[i] + ref[...].astype(F32)).astype(BF16)

    return chain_call(
        "share",
        body,
        after,
        [kept, *came],
        [three, one, one, one],
        jax.ShapeDtypeStruct((3, M, width), BF16),
        half_specs(M, width, 0)[0],
        grid=(2,),
    )


def pointwise_call(kept, came, k, chip, after):
    _, M, width = chip.shape
    three, one = half_specs(M, width, k)
    three_out, one_out = half_specs(M, width, 0)

    def body(kept_ref, gate, up, back, chip_ref, *outs):
        for at in range(0, width // 2, 128):
            cut = slice(at, at + 128)
            sums = [
                kept_ref[i, :, cut] + ref[:, cut].astype(F32) + chip_ref[i, :, cut].astype(F32)
                for i, ref in enumerate((gate, up, back))
            ]
            for out, value in zip(outs, pointwise(*sums)):
                out[:, cut] = value

    return chain_call(
        "point",
        body,
        after,
        [kept, *came, chip],
        [three, one, one, one, three_out],
        [jax.ShapeDtypeStruct((M, width), BF16)] * 3,
        [one_out] * 3,
        grid=(2,),
    )


def results_specs(hs, t0, n, mode):
    specs = []
    for h in hs:
        m = h[0].shape[0]
        specs += [pl.BlockSpec((m, T), lambda j: (0, t0 + jnp.minimum(j, n - 1)), pipeline_mode=mode)] * 3
        specs += [pl.BlockSpec((m, T), lambda j: (0, t0 + jnp.maximum(j - n, 0)), pipeline_mode=mode)] * 3
    return specs


def each_half(n, refs, work):
    j = pl.program_id(0)

    def rows(lo):
        return [
            jnp.concatenate([refs[at + lo + k][...] for at in range(0, len(refs), 6)], axis=0)
            for k in range(3)
        ]

    @pl.when(j < n)
    def _():
        work(*rows(0))

    @pl.when(j >= n)
    def _():
        work(*rows(3))


def backward_call(core, weights, span, hs, dtypes, after):
    t0, n = span
    F = weights[0].shape[0]
    tiles = weights[0].shape[1] // T // 2
    M = hs[0][0].shape[0]
    R = M * len(hs)

    def body(s, wg_hbm, wu_hbm, wd_hbm, *refs):
        h_hbm = refs[: 6 * len(hs)]
        *outs, acc = refs[6 * len(hs) :]
        tile = tile_of(s[0], tiles, t0, n)
        acc[...] = jnp.zeros_like(acc)

        def step(wg, wu, wd, *h):
            def work(hid, dg, du):
                acc[0] += jnp.dot(hid, wd[...], preferred_element_type=F32)
                acc[1] += lax.dot_general(
                    dg, wg[...], NT, preferred_element_type=F32
                ) + lax.dot_general(du, wu[...], NT, preferred_element_type=F32)

            each_half(n, h, work)

        pltpu.emit_pipeline(
            step,
            grid=(2 * n,),
            in_specs=weight_specs(tile, F, DEEP) + results_specs(hs, t0, n, DEEP),
        )(wg_hbm, wu_hbm, wd_hbm, *h_hbm)
        for k, out in enumerate(outs):
            out[...] = acc[:, k * M : (k + 1) * M].astype(out.dtype)

    flat = [v for h in hs for v in h]
    return chain_call(
        "back",
        body,
        after,
        [core, *weights, *flat],
        [SMEM] + [ANY] * (3 + len(flat)),
        [jax.ShapeDtypeStruct((2, M, F), dtype) for dtype in dtypes],
        [VMEM] * len(hs),
        [pltpu.VMEM((2, R, F), F32)],
    )


def join_call(part, came, split, after):
    _, M, F = part.shape
    both = pl.BlockSpec((2, M // 2, F), lambda j: (0, j, 0))

    def body(part_ref, came_ref, *outs):
        for i in range(2):
            value = (part_ref[i] + came_ref[i].astype(F32)).astype(BF16)
            if split:
                outs[i][...] = value
            else:
                outs[0][i] = value

    if split:
        shapes, specs = [(M, F)] * 2, [pl.BlockSpec((M // 2, F), lambda j: (j, 0))] * 2
    else:
        shapes, specs = [(2, M, F)], [both]
    return chain_call(
        "join",
        body,
        after,
        [part, came],
        [both, both],
        [jax.ShapeDtypeStruct(shape, BF16) for shape in shapes],
        specs,
        grid=(2,),
    )


def grads_call(core, span, rows, hs, shapes, after):
    t0, n = span
    R = len(rows)
    M, F = rows[0][0].shape[-2:]
    held = [v for some in rows for v in some]
    tiles = shapes[0][1] // T // 2

    def body(s, *refs):
        h_hbm = refs[len(held) : len(held) + 6 * R]
        gate_hbm, up_hbm, down_hbm, x_rows, c_rows, x_in, sem = refs[len(held) + 6 * R :]
        tile = tile_of(s[0], tiles, t0, n)
        copies = []
        at = 0
        for k, some in enumerate(rows):
            x, c = (refs[at], refs[at + 1]) if len(some) == 2 else (refs[at].at[0], refs[at].at[1])
            at += len(some)
            copies.append(pltpu.make_async_copy(x, x_in.at[k], sem.at[k]))
            copies.append(pltpu.make_async_copy(c, c_rows.at[pl.ds(k * M, M)], sem.at[R + k]))
        for copy in copies[::2] + copies[1::2]:
            copy.start()
        for k in range(R):
            copies[2 * k].wait()
            x_rows[:, k * M : (k + 1) * M] = x_in[k].T
        for copy in copies[1::2]:
            copy.wait()

        def step(*h):
            h, (gate, up, down) = h[:-3], h[-3:]

            def work(hid, dg, du):
                gate[...] = jnp.dot(x_rows[...], dg, preferred_element_type=F32).astype(BF16)
                up[...] = jnp.dot(x_rows[...], du, preferred_element_type=F32).astype(BF16)
                down[...] = lax.dot_general(
                    hid, c_rows[...], TN, preferred_element_type=F32
                ).astype(BF16)

            each_half(n, h, work)

        pltpu.emit_pipeline(
            step,
            grid=(2 * n,),
            in_specs=results_specs(hs, t0, n, DEEP),
            out_specs=weight_specs(tile, F, None),
        )(*h_hbm, gate_hbm, up_hbm, down_hbm)

    flat = [v for h in hs for v in h]
    return chain_call(
        "grads",
        body,
        after,
        [core, *held, *flat],
        [SMEM] + [ANY] * (len(held) + len(flat)),
        [jax.ShapeDtypeStruct(s, BF16) for s in shapes],
        [ANY] * 3,
        [
            pltpu.VMEM((F, R * M), BF16),
            pltpu.VMEM((R * M, F), BF16),
            pltpu.VMEM((R, M, F), BF16),
            pltpu.SemaphoreType.DMA((2 * R,)),
        ],
    )


ORDER = ["S0", "A0", "W1", "S1", "A1", "W2", "S2", "P0", "A2", "S3", "P1", "A3", "B01", "P2", "B2"]
ORDER += ["J2", "P3", "B3", "J3", "G", "J0"]


def tiled(rows, cols):
    def local(inputs, cotangent, w_gate, w_up, w_down):
        weights = (w_gate, w_up, w_down)
        shapes = [w.shape for w in weights]
        full = (0, w_gate.shape[1] // T // 2)
        core = (lax.axis_index("col") % 2).astype(jnp.int32).reshape(1)
        to_core = lambda v: lax.ppermute(v, "col", [(i, i ^ 1) for i in range(cols)])
        to_chip = lambda v: lax.ppermute(v, "col", [(i, i ^ 2) for i in range(cols)])
        onward = lambda v: lax.ppermute(v, "row", [(i, (i + 1) % rows) for i in range(rows)])
        last = [None]

        def then(call, *args):
            out = call(*args, last[0])
            last[0] = out[0] if isinstance(out, (list, tuple)) else out
            return out

        held = [(inputs, cotangent), (onward(jnp.stack([inputs, cotangent])),)]

        M = inputs.shape[0]
        kept, came, block, chip, h, totals = {}, {}, {}, {}, {}, {}
        for word in ORDER:
            step, digits = word[0], [int(d) for d in word[1:]]
            k = digits[0] if digits else None
            if step == "S":
                *sent, own = then(forward_call, core, weights, [held[k] for k in digits])
                sent = [to_core(v) for v in sent]
                for at, k in enumerate(digits):
                    kept[k], came[k], block[k] = own, sent, at
            elif step == "W":
                held[k] = (then(hold_call, held[k][0]),)
                held.append((onward(held[k][0]),))
            elif step == "A":
                chip[k] = to_chip(then(add_call, kept[k], came[k], block[k], M))
            elif step == "P":
                own = then(pointwise_call, kept[k], came[k], block[k], chip[k])
                h[k] = [to_core(v) for v in own] + list(own)
            elif step == "B":
                dtypes = [BF16 if k == 1 else F32 for k in digits]
                sums = then(backward_call, core, weights, full, [h[k] for k in digits], dtypes)
                totals.update(zip(digits, sums))
                if 1 in digits:
                    moving = onward(totals[1])
            elif step == "J" and k:
                moving = onward(*then(join_call, totals[k], moving, False))
            elif step == "J":
                output, d_inputs = then(join_call, totals[0], moving, True)
            elif step == "G":
                grads = then(grads_call, core, full, held, [h[k] for k in range(rows)], shapes)
        return (output, d_inputs, *grads)

    return local


def plain(inputs, cotangent, w_gate, w_up, w_down):
    full_inputs, full_cotangent = (
        lax.all_gather(inputs, "row", axis=0, tiled=True),
        lax.all_gather(cotangent, "row", axis=0, tiled=True),
    )
    hidden_width = w_gate.shape[1]
    feature_width = w_down.shape[1]
    gate_part = jnp.dot(full_inputs, w_gate, preferred_element_type=F32)
    up_part = jnp.dot(full_inputs, w_up, preferred_element_type=F32)
    back_grad = lax.dot_general(full_cotangent, w_down, NT, preferred_element_type=F32)
    shares = lax.psum_scatter(
        jnp.concatenate([gate_part, up_part, back_grad], axis=1),
        "col",
        scatter_dimension=0,
        tiled=True,
    )
    hidden, d_gate, d_up = (
        lax.all_gather(share, "col", axis=0, tiled=True)
        for share in pointwise(
            shares[:, :hidden_width],
            shares[:, hidden_width : 2 * hidden_width],
            shares[:, 2 * hidden_width :],
        )
    )
    grad_down = lax.dot_general(hidden, full_cotangent, TN, preferred_element_type=F32)
    grad_gate = lax.dot_general(full_inputs, d_gate, TN, preferred_element_type=F32)
    grad_up = lax.dot_general(full_inputs, d_up, TN, preferred_element_type=F32)
    forward_term = jnp.dot(hidden, w_down, preferred_element_type=F32)
    back_term = lax.dot_general(d_gate, w_gate, NT, preferred_element_type=F32)
    back_term = back_term + lax.dot_general(d_up, w_up, NT, preferred_element_type=F32)
    results = lax.psum_scatter(
        jnp.concatenate([forward_term, back_term], axis=1), "row", scatter_dimension=0, tiled=True
    )
    return (
        results[:, :feature_width].astype(BF16),
        results[:, feature_width:].astype(BF16),
        grad_gate.astype(BF16),
        grad_up.astype(BF16),
        grad_down.astype(BF16),
    )


def solution(mesh):
    rows, cols = mesh.shape["row"], mesh.shape["col"]

    def local(inputs, cotangent, w_gate, w_up, w_down):
        step = plain
        if rows == 4 and cols == 4 and w_gate.shape[1] % (14 * T) == 0 and inputs.shape[0] % 16 == 0:
            step = tiled(rows, cols)
        return step(inputs, cotangent, w_gate, w_up, w_down)

    return jax.shard_map(
        local,
        mesh=mesh,
        in_specs=(
            P(("groups", "row"), "col"),
            P(("groups", "row"), "col"),
            P("col", "row"),
            P("col", "row"),
            P("row", "col"),
        ),
        out_specs=(
            P(("groups", "row"), "col"),
            P(("groups", "row"), "col"),
            P(("groups", "col"), "row"),
            P(("groups", "col"), "row"),
            P(("groups", "row"), "col"),
        ),
        check_vma=False,
    )
```
